32 devices in a mesh: tm: 4 (over y, core), height: 8 (over z, x).
Axes of the slice: x: 2, y: 2, z: 4, core: 2. Of those that a mesh axis runs over, the one named last changes fastest.
Arguments:
- hidden_in: bfloat16 [8, 64, 128, 192], P('tm', 'height'), may hold values from -6 to 6
- gain_first: float32 [192], replicated, may hold values from 0.5 to 2
- weight_first: bfloat16 [3, 3, 3, 192, 192], replicated, may hold values from -0.078125 to 0.078125
- bias_first: float32 [192], replicated, may hold values from -3 to 3
- gain_second: float32 [192], replicated, may hold values from 0.5 to 2
- weight_second: bfloat16 [3, 3, 3, 192, 192], replicated, may hold values from -0.078125 to 0.078125
- bias_second: float32 [192], replicated, may hold values from -3 to 3
Outputs:
- block_out: bfloat16 [8, 64, 128, 192], P('tm', 'height')
The draws below stay inside these ranges and needn't reach their ends.
All inputs are finite; a program needn't handle non-finite values.
Results may differ from the reference program's by a relative error of at most 0.0042.
Values may be sent and summed in bfloat16 or wider, within the bound.
A program may use at most 64 MiB of HBM per device.

```python
import math
import jax
import jax.numpy as jnp
from jax import lax

C = 192
WIDTH = 128
FRAMES = 8
ROWS = 64


def levels(own_key, dims, cuts, smallest, top_value):
    level = 1.0
    for dim, parts in cuts:
        heights = jax.random.uniform(jax.random.fold_in(jax.random.fold_in(own_key, 6), dim), (parts,), jnp.float32, smallest / len(cuts), top_value / len(cuts))
        level = level * jnp.repeat(jnp.exp(heights), dims[dim] // parts).reshape((-1,) + (1,) * (len(dims) - 1 - dim))
    return level


def normal_values(rng, dims, deviation, most, cuts=(), kind=jnp.bfloat16):
    drawn = deviation * jax.random.normal(rng, dims, jnp.float32)
    if cuts:
        drawn = drawn * levels(rng, dims, cuts, -0.22, 0.18)
    return jnp.clip(drawn, -most, most).astype(kind)


def setup_inputs(seed: int = 0) -> dict:
    splits = jax.random.split(jax.random.key(seed), 8)
    return {
        "hidden_in": normal_values(splits[0], (FRAMES, ROWS, WIDTH, C), 1.0, 6.0, ((0, 4), (1, 8))),
        "gain_first": jnp.clip(jnp.exp(jax.random.uniform(splits[1], (C,), jnp.float32, math.log(0.5), math.log(2.0))), 0.5, 2.0),
        "weight_first": normal_values(splits[2], (3, 3, 3, C, C), (27 * C) ** -0.5, 0.078125),
        "bias_first": normal_values(splits[3], (C,), 0.5, 3.0, (), jnp.float32),
        "gain_second": jnp.clip(jnp.exp(jax.random.uniform(splits[4], (C,), jnp.float32, math.log(0.5), math.log(2.0))), 0.5, 2.0),
        "weight_second": normal_values(splits[5], (3, 3, 3, C, C), (27 * C) ** -0.5, 0.078125),
        "bias_second": normal_values(splits[6], (C,), 0.5, 3.0, (), jnp.float32),
    }


epsilon = 1e-06

def normalize(values, gain):
    values = values.astype(jnp.float32)
    scaled = values * lax.rsqrt(lax.optimization_barrier(jnp.mean(values * values, axis=-1, keepdims=True)) + epsilon) * gain
    return jax.nn.silu(scaled).astype(jnp.bfloat16)

def window_sum(padded, weight, frames, rows, width):
    channels = padded.shape[-1]
    summed = jnp.zeros((frames * rows * width, channels), jnp.float32)
    for time_tap in range(3):
        pieces = [padded[time_tap:time_tap + frames, row_tap:row_tap + rows, col_tap:col_tap + width] for row_tap in range(3) for col_tap in range(3)]
        columns = jnp.concatenate(pieces, axis=-1).reshape(frames * rows * width, 9 * channels)
        summed = summed + jnp.dot(columns, weight[time_tap].reshape(9 * channels, channels), preferred_element_type=jnp.float32)
    return summed.reshape(frames, rows, width, channels)

def convolve(activated, weight, bias):
    frames, rows, width, channels = activated.shape
    padded = jnp.pad(activated, ((2, 0), (1, 1), (1, 1), (0, 0)))

    def frame_out(frame_at):
        block_in = lax.dynamic_slice_in_dim(padded, frame_at, 3, 0)
        return window_sum(block_in, weight, 1, rows, width)[0] + bias
    return lax.map(frame_out, jnp.arange(frames, dtype=jnp.int32))

def reference(hidden_in, gain_first, weight_first, bias_first, gain_second, weight_second, bias_second):
    first_act = normalize(hidden_in, gain_first)
    middle = convolve(first_act, weight_first, bias_first)
    second_act = normalize(middle, gain_second)
    result = hidden_in.astype(jnp.float32) + convolve(second_act, weight_second, bias_second)
    return result.astype(jnp.bfloat16)
```

```python
import functools

import jax
import jax.numpy as jnp
from jax import lax
from jax.experimental import pallas as pl
from jax.experimental.pallas import tpu as pltpu
from jax.sharding import PartitionSpec as P

epsilon = 1e-06
MESH = pl.DeviceIdType.MESH
CHUNK = 4


def normalize(values, gain):
    scaled = values * lax.rsqrt(jnp.mean(values * values, axis=-1, keepdims=True) + epsilon) * gain
    return jax.nn.silu(scaled).astype(jnp.bfloat16)


def kernel(
    tms, heights, x_ref, g1_ref, b1_ref, g2_ref, b2_ref, w1_hbm, w2_hbm, o_ref,
    ext1, ext2, acc, w1, w2, wsem, t_send, t_recv, h_send, h_recv,
):
    frames, rows, width, chans = x_ref.shape
    chunks = rows // CHUNK
    tm, ht = lax.axis_index("tm"), lax.axis_index("height")
    has_prev, has_next = tm > 0, tm < tms - 1
    has_up, has_down = ht > 0, ht < heights - 1

    load1 = pltpu.make_async_copy(w1_hbm, w1, wsem.at[0])
    load2 = pltpu.make_async_copy(w2_hbm, w2, wsem.at[1])
    load1.start()
    load2.start()

    barrier = pltpu.get_barrier_semaphore()
    sides = ((has_prev, {"tm": tm - 1}), (has_next, {"tm": tm + 1}), (has_up, {"height": ht - 1}), (has_down, {"height": ht + 1}))
    for there, who in sides:
        @pl.when(there)
        def _(who=who):
            pl.semaphore_signal(barrier, inc=1, device_id=who, device_id_type=MESH)

    zeros_row = jnp.zeros((width, chans), jnp.bfloat16)
    for ext in (ext1, ext2):
        @pl.when(jnp.logical_not(has_prev))
        def _(ext=ext):
            for f in range(2):
                @pl.loop(0, rows + 2)
                def _(r, f=f):
                    ext[f, r] = zeros_row

        @pl.when(jnp.logical_not(has_up))
        def _(ext=ext):
            for f in range(frames + 2):
                ext[f, 0] = zeros_row

        @pl.when(jnp.logical_not(has_down))
        def _(ext=ext):
            for f in range(frames + 2):
                ext[f, rows + 1] = zeros_row

    pl.semaphore_wait(barrier, sum(there.astype(jnp.int32) for there, _ in sides))

    exts = (ext1, ext2)

    def time_copy(p, f, c):
        lines = pl.ds(1 + c * CHUNK, CHUNK)
        return pltpu.make_async_remote_copy(
            src_ref=exts[p].at[frames + f, lines], dst_ref=exts[p].at[f, lines],
            send_sem=t_send.at[p, f, c], recv_sem=t_recv.at[p, f, c],
            device_id={"tm": tm + 1}, device_id_type=MESH)

    def row_copy(p, f, down):
        src, dst, who = (rows, 0, ht + 1) if down else (1, rows + 1, ht - 1)
        return pltpu.make_async_remote_copy(
            src_ref=exts[p].at[f, src], dst_ref=exts[p].at[f, dst],
            send_sem=h_send.at[p, f, int(down)], recv_sem=h_recv.at[p, f, int(down)],
            device_id={"height": who}, device_id_type=MESH)

    def when_start(cond, copy):
        @pl.when(cond)
        def _():
            copy.start()

    def when_recv(cond, copy):
        @pl.when(cond)
        def _():
            copy.wait_recv()

    def when_sent(cond, copy):
        @pl.when(cond)
        def _():
            copy.wait_send()

    def send_part(p, f, c):
        if c == 0:
            when_start(has_up, row_copy(p, f + 2, False))
        if c == chunks - 1:
            when_start(has_down, row_copy(p, f + 2, True))
        if f >= frames - 2:
            when_start(has_next, time_copy(p, f - (frames - 2), c))

    def contrib(ext, w, o, taps, first):
        @pl.loop(0, chunks)
        def _(c):
            r0 = c * CHUNK
            for k in range(3):
                total = None
                for t in taps:
                    for j in range(3):
                        lines = ext[o + t, pl.ds(r0 + j, CHUNK)].reshape(CHUNK * width, chans)
                        part = jnp.dot(lines, w[t, j, k], preferred_element_type=jnp.float32)
                        total = part if total is None else total + part
                total = total.reshape(CHUNK, width, chans)
                if first:
                    acc[k, o, pl.ds(r0, CHUNK)] = total
                else:
                    acc[k, o, pl.ds(r0, CHUNK)] += total

    at_col = lax.broadcasted_iota(jnp.int32, (width, chans), 0)

    def combined(o, r, bias):
        left = jnp.where(at_col == 0, 0.0, pltpu.roll(acc[0, o, r], 1, 0))
        right = jnp.where(at_col == width - 1, 0.0, pltpu.roll(acc[2, o, r], width - 1, 0))
        return acc[1, o, r] + left + right + bias

    def convolve(p, w, finish):
        ext = exts[p]
        for f in range(2, frames + 2):
            when_recv(has_up, row_copy(p, f, True))
            when_recv(has_down, row_copy(p, f, False))
        for o in range(frames):
            contrib(ext, w, o, tuple(t for t in range(3) if o + t >= 2), True)
        for f in range(2):
            for c in range(chunks):
                when_recv(has_prev, time_copy(p, f, c))
                if c == 0:
                    when_start(has_prev & has_up, row_copy(p, f, False))
                if c == chunks - 1:
                    when_start(has_prev & has_down, row_copy(p, f, True))
        for f in range(2):
            when_recv(has_prev & has_up, row_copy(p, f, True))
            when_recv(has_prev & has_down, row_copy(p, f, False))
        for o in range(min(frames, 2)):
            contrib(ext, w, o, tuple(t for t in range(3) if o + t < 2), False)
        for c in range(chunks):
            for o in range(frames):
                finish(o, c)

    for c in range(chunks):
        for f in range(frames):
            @pl.loop(c * CHUNK, (c + 1) * CHUNK)
            def _(r, f=f):
                ext1[f + 2, r + 1] = normalize(x_ref[f, r].astype(jnp.float32), g1_ref[...])
            send_part(0, f, c)

    def finish_first(o, c):
        @pl.loop(c * CHUNK, (c + 1) * CHUNK)
        def _(r):
            ext2[o + 2, r + 1] = normalize(combined(o, r, b1_ref[...]), g2_ref[...])
        send_part(1, o, c)

    def finish_second(o, c):
        @pl.loop(c * CHUNK, (c + 1) * CHUNK)
        def _(r):
            o_ref[o, r] = (x_ref[o, r].astype(jnp.float32) + combined(o, r, b2_ref[...])).astype(jnp.bfloat16)

    load1.wait()
    convolve(0, w1, finish_first)
    load2.wait()
    convolve(1, w2, finish_second)

    for p in range(2):
        for f in range(2):
            for c in range(chunks):
                when_sent(has_next, time_copy(p, f, c))
        for f in range(frames + 2):
            extra = has_prev if f < 2 else True
            when_sent(has_up & extra, row_copy(p, f, False))
            when_sent(has_down & extra, row_copy(p, f, True))


def local(tms, heights, hidden_in, gain_first, weight_first, bias_first, gain_second, weight_second, bias_second):
    frames, rows, width, chans = hidden_in.shape
    chunks = rows // CHUNK
    vmem = pl.BlockSpec(memory_space=pltpu.VMEM)
    hbm = pl.BlockSpec(memory_space=pl.ANY)
    ext = pltpu.VMEM((frames + 2, rows + 2, width, chans), jnp.bfloat16)
    weight = pltpu.VMEM(weight_first.shape, jnp.bfloat16)
    dma = pltpu.SemaphoreType.DMA
    flops = 2 * 2 * frames * rows * width * 27 * chans * chans
    return pl.pallas_call(
        functools.partial(kernel, tms, heights),
        out_shape=jax.ShapeDtypeStruct(hidden_in.shape, jnp.bfloat16),
        in_specs=[vmem] * 5 + [hbm] * 2,
        out_specs=vmem,
        scratch_shapes=[
            ext,
            ext,
            pltpu.VMEM((3, frames, rows, width, chans), jnp.float32),
            weight,
            weight,
            dma((2,)),
            dma((2, 2, chunks)),
            dma((2, 2, chunks)),
            dma((2, frames + 2, 2)),
            dma((2, frames + 2, 2)),
        ],
        compiler_params=pltpu.CompilerParams(
            collective_id=0, has_side_effects=True, vmem_limit_bytes=48 * 2**20
        ),
        cost_estimate=pl.CostEstimate(flops=flops, bytes_accessed=8 * 2**20, transcendentals=0),
    )(
        hidden_in,
        gain_first.reshape(1, chans),
        bias_first.reshape(1, chans),
        gain_second.reshape(1, chans),
        bias_second.reshape(1, chans),
        weight_first,
        weight_second,
    )


def solution(mesh):
    in_specs = (P("tm", "height", None, None), P(), P(), P(), P(), P(), P())
    out_specs = P("tm", "height", None, None)
    body = functools.partial(local, mesh.shape["tm"], mesh.shape["height"])
    return jax.shard_map(body, mesh=mesh, in_specs=in_specs, out_specs=out_specs, check_vma=False)
```

```python
import functools

import jax
import jax.numpy as jnp
from jax import lax
from jax.experimental import pallas as pl
from jax.experimental.pallas import tpu as pltpu
from jax.sharding import PartitionSpec as P

epsilon = 1e-06
MESH = pl.DeviceIdType.MESH
CHUNK = 4


def normalize(values, gain):
    scaled = values * lax.rsqrt(jnp.mean(values * values, axis=0, keepdims=True) + epsilon) * gain
    return jax.nn.silu(scaled).astype(jnp.bfloat16)


def kernel(
    tms, heights, x_ref, g1_ref, b1_ref, g2_ref, b2_ref, w1_hbm, w2_hbm, o_ref,
    ext1, ext2, acc, w1, w2, turned, vecs, vsem, wsem, t_send, t_recv, h_send, h_recv,
):
    frames, rows, chans, width = x_ref.shape
    chunks = rows // CHUNK
    tm, ht = lax.axis_index("tm"), lax.axis_index("height")
    has_prev, has_next = tm > 0, tm < tms - 1
    has_up, has_down = ht > 0, ht < heights - 1

    load1 = pltpu.make_async_copy(w1_hbm, w1, wsem.at[0])
    load2 = pltpu.make_async_copy(w2_hbm, w2, wsem.at[1])
    load1.start()
    load2.start()
    small = [pltpu.make_async_copy(ref, vecs.at[i], vsem.at[i]) for i, ref in enumerate((g1_ref, b1_ref, g2_ref, b2_ref))]
    for copy in small:
        copy.start()

    barrier = pltpu.get_barrier_semaphore()
    sides = ((has_prev, {"tm": tm - 1}), (has_next, {"tm": tm + 1}), (has_up, {"height": ht - 1}), (has_down, {"height": ht + 1}))
    for there, who in sides:
        @pl.when(there)
        def _(who=who):
            pl.semaphore_signal(barrier, inc=1, device_id=who, device_id_type=MESH)

    zeros_row = jnp.zeros((chans, width), jnp.bfloat16)
    for ext in (ext1, ext2):
        @pl.when(jnp.logical_not(has_prev))
        def _(ext=ext):
            for f in range(2):
                @pl.loop(0, rows + 2)
                def _(r, f=f):
                    ext[f, r] = zeros_row

        @pl.when(jnp.logical_not(has_up))
        def _(ext=ext):
            for f in range(frames + 2):
                ext[f, 0] = zeros_row

        @pl.when(jnp.logical_not(has_down))
        def _(ext=ext):
            for f in range(frames + 2):
                ext[f, rows + 1] = zeros_row

    pl.semaphore_wait(barrier, sum(there.astype(jnp.int32) for there, _ in sides))

    exts = (ext1, ext2)

    def time_copy(p, f, c):
        lines = pl.ds(1 + c * CHUNK, CHUNK)
        return pltpu.make_async_remote_copy(
            src_ref=exts[p].at[frames + f, lines], dst_ref=exts[p].at[f, lines],
            send_sem=t_send.at[p, f, c], recv_sem=t_recv.at[p, f, c],
            device_id={"tm": tm + 1}, device_id_type=MESH)

    def row_copy(p, f, down):
        src, dst, who = (rows, 0, ht + 1) if down else (1, rows + 1, ht - 1)
        return pltpu.make_async_remote_copy(
            src_ref=exts[p].at[f, src], dst_ref=exts[p].at[f, dst],
            send_sem=h_send.at[p, f, int(down)], recv_sem=h_recv.at[p, f, int(down)],
            device_id={"height": who}, device_id_type=MESH)

    def when_start(cond, copy):
        @pl.when(cond)
        def _():
            copy.start()

    def when_recv(cond, copy):
        @pl.when(cond)
        def _():
            copy.wait_recv()

    def when_sent(cond, copy):
        @pl.when(cond)
        def _():
            copy.wait_send()

    def send_part(p, f, c):
        if c == 0:
            when_start(has_up, row_copy(p, f + 2, False))
        if c == chunks - 1:
            when_start(has_down, row_copy(p, f + 2, True))
        if f >= frames - 2:
            when_start(has_next, time_copy(p, f - (frames - 2), c))

    def turn(w):
        square = (chans, chans)
        same = lax.broadcasted_iota(jnp.int32, square, 0) == lax.broadcasted_iota(jnp.int32, square, 1)
        identity = same.astype(jnp.float32).astype(jnp.bfloat16)

        @pl.loop(0, 3)
        def _(t):
            for k in range(3):
                taps = jnp.concatenate([w[t, j, k] for j in range(3)], axis=0)
                flipped = lax.dot_general(identity, taps, (((1,), (1,)), ((), ())), preferred_element_type=jnp.float32)
                turned[t, k * chans:(k + 1) * chans, :] = flipped.astype(jnp.bfloat16)

    def contrib(ext, o, taps, first):
        @pl.loop(0, chunks)
        def _(c):
            r0 = c * CHUNK
            total = None
            for t in taps:
                lines = [ext[o + t, r0 + i] for i in range(CHUNK + 2)]
                block = jnp.concatenate([jnp.concatenate(lines[j:j + CHUNK], axis=1) for j in range(3)], axis=0)
                part = jnp.dot(turned[t], block, preferred_element_type=jnp.float32)
                total = part if total is None else total + part
            if first:
                acc[o, c] = total
            else:
                acc[o, c] += total

    at_col = lax.broadcasted_iota(jnp.int32, (chans, width), 1)

    def combined(o, c, i, bias):
        cols = slice(i * width, (i + 1) * width)
        left = jnp.where(at_col == 0, 0.0, pltpu.roll(acc[o, c, 0:chans, cols], 1, 1))
        right = jnp.where(at_col == width - 1, 0.0, pltpu.roll(acc[o, c, 2 * chans:3 * chans, cols], width - 1, 1))
        return acc[o, c, chans:2 * chans, cols] + left + right + bias

    def convolve(p, w, finish):
        ext = exts[p]
        turn(w)
        for f in range(2, frames + 2):
            when_recv(has_up, row_copy(p, f, True))
            when_recv(has_down, row_copy(p, f, False))
        for o in range(frames):
            contrib(ext, o, tuple(t for t in range(3) if o + t >= 2), True)
        for f in range(2):
            for c in range(chunks):
                when_recv(has_prev, time_copy(p, f, c))
                if c == 0:
                    when_start(has_prev & has_up, row_copy(p, f, False))
                if c == chunks - 1:
                    when_start(has_prev & has_down, row_copy(p, f, True))
        for f in range(2):
            when_recv(has_prev & has_up, row_copy(p, f, True))
            when_recv(has_prev & has_down, row_copy(p, f, False))
        for o in range(min(frames, 2)):
            contrib(ext, o, tuple(t for t in range(3) if o + t < 2), False)
        for c in range(chunks):
            for o in range(frames):
                finish(o, c)

    for copy in small:
        copy.wait()
    square = (chans, chans)
    diagonal = lax.broadcasted_iota(jnp.int32, square, 0) == lax.broadcasted_iota(jnp.int32, square, 1)
    gain1, bias1, gain2, bias2 = [
        jnp.sum(jnp.where(diagonal, vecs[i], 0.0), axis=1, keepdims=True) for i in range(4)
    ]
    for c in range(chunks):
        for f in range(frames):
            @pl.loop(c * CHUNK, (c + 1) * CHUNK)
            def _(r, f=f):
                ext1[f + 2, r + 1] = normalize(x_ref[f, r].astype(jnp.float32), gain1)
            send_part(0, f, c)

    def finish_first(o, c):
        for i in range(CHUNK):
            ext2[o + 2, c * CHUNK + i + 1] = normalize(combined(o, c, i, bias1), gain2)
        send_part(1, o, c)

    def finish_second(o, c):
        for i in range(CHUNK):
            r = c * CHUNK + i
            o_ref[o, r] = (x_ref[o, r].astype(jnp.float32) + combined(o, c, i, bias2)).astype(jnp.bfloat16)

    load1.wait()
    convolve(0, w1, finish_first)
    load2.wait()
    convolve(1, w2, finish_second)

    for p in range(2):
        for f in range(2):
            for c in range(chunks):
                when_sent(has_next, time_copy(p, f, c))
        for f in range(frames + 2):
            extra = has_prev if f < 2 else True
            when_sent(has_up & extra, row_copy(p, f, False))
            when_sent(has_down & extra, row_copy(p, f, True))


def local(tms, heights, hidden_in, gain_first, weight_first, bias_first, gain_second, weight_second, bias_second):
    frames, rows, width, chans = hidden_in.shape
    chunks = rows // CHUNK
    vmem = pl.BlockSpec(memory_space=pltpu.VMEM)
    hbm = pl.BlockSpec(memory_space=pl.ANY)
    ext = pltpu.VMEM((frames + 2, rows + 2, chans, width), jnp.bfloat16)
    weight = pltpu.VMEM(weight_first.shape, jnp.bfloat16)
    dma = pltpu.SemaphoreType.DMA
    flops = 2 * 2 * frames * rows * width * 27 * chans * chans
    turned_in = jnp.swapaxes(hidden_in, 2, 3)
    result = pl.pallas_call(
        functools.partial(kernel, tms, heights),
        out_shape=jax.ShapeDtypeStruct(turned_in.shape, jnp.bfloat16),
        in_specs=[vmem] + [hbm] * 6,
        out_specs=vmem,
        scratch_shapes=[
            ext,
            ext,
            pltpu.VMEM((frames, chunks, 3 * chans, CHUNK * width), jnp.float32),
            weight,
            weight,
            pltpu.VMEM((3, 3 * chans, 3 * chans), jnp.bfloat16),
            pltpu.VMEM((4, 1, chans), jnp.float32),
            dma((4,)),
            dma((2,)),
            dma((2, 2, chunks)),
            dma((2, 2, chunks)),
            dma((2, frames + 2, 2)),
            dma((2, frames + 2, 2)),
        ],
        compiler_params=pltpu.CompilerParams(
            collective_id=0, has_side_effects=True, vmem_limit_bytes=56 * 2**20
        ),
        cost_estimate=pl.CostEstimate(flops=flops, bytes_accessed=8 * 2**20, transcendentals=0),
    )(
        turned_in,
        gain_first.reshape(1, chans),
        bias_first.reshape(1, chans),
        gain_second.reshape(1, chans),
        bias_second.reshape(1, chans),
        weight_first,
        weight_second,
    )
    return jnp.swapaxes(result, 2, 3)


def solution(mesh):
    in_specs = (P("tm", "height", None, None), P(), P(), P(), P(), P(), P())
    out_specs = P("tm", "height", None, None)
    body = functools.partial(local, mesh.shape["tm"], mesh.shape["height"])
    return jax.shard_map(body, mesh=mesh, in_specs=in_specs, out_specs=out_specs, check_vma=False)
```

```python
import functools

import jax
import jax.numpy as jnp
from jax import lax
from jax.experimental import pallas as pl
from jax.experimental.pallas import tpu as pltpu
from jax.sharding import PartitionSpec as P

epsilon = 1e-06
MESH = pl.DeviceIdType.MESH
CHUNK = 4


def normalize(values, gain):
    scaled = values * lax.rsqrt(jnp.mean(values * values, axis=0, keepdims=True) + epsilon) * gain
    return jax.nn.silu(scaled).astype(jnp.bfloat16)


def kernel(
    tms, heights, x_ref, g1_ref, b1_ref, g2_ref, b2_ref, w1_hbm, w2_hbm, o_ref,
    ext1, ext2, acc, w1, w2, turned, vecs, vsem, wsem, t_send, t_recv, h_send, h_recv,
):
    frames, rows, chans, width = x_ref.shape
    chunks = rows // CHUNK
    tm, ht = lax.axis_index("tm"), lax.axis_index("height")
    has_prev, has_next = tm > 0, tm < tms - 1
    has_up, has_down = ht > 0, ht < heights - 1

    load1 = pltpu.make_async_copy(w1_hbm, w1, wsem.at[0])
    load2 = pltpu.make_async_copy(w2_hbm, w2, wsem.at[1])
    load1.start()
    small = [pltpu.make_async_copy(ref, vecs.at[i], vsem.at[i]) for i, ref in enumerate((g1_ref, b1_ref, g2_ref, b2_ref))]
    for copy in small:
        copy.start()

    barrier = pltpu.get_barrier_semaphore()
    sides = ((has_prev, {"tm": tm - 1}), (has_next, {"tm": tm + 1}), (has_up, {"height": ht - 1}), (has_down, {"height": ht + 1}))
    for there, who in sides:
        @pl.when(there)
        def _(who=who):
            pl.semaphore_signal(barrier, inc=1, device_id=who, device_id_type=MESH)

    zeros_row = jnp.zeros((chans, width), jnp.bfloat16)
    for ext in (ext1, ext2):
        @pl.when(jnp.logical_not(has_prev))
        def _(ext=ext):
            for f in range(2):
                @pl.loop(0, rows + 2)
                def _(r, f=f):
                    ext[f, r] = zeros_row

        @pl.when(jnp.logical_not(has_up))
        def _(ext=ext):
            for f in range(frames + 2):
                ext[f, 0] = zeros_row

        @pl.when(jnp.logical_not(has_down))
        def _(ext=ext):
            for f in range(frames + 2):
                ext[f, rows + 1] = zeros_row


    exts = (ext1, ext2)

    def time_copy(p, f, c):
        lines = pl.ds(1 + c * CHUNK, CHUNK)
        return pltpu.make_async_remote_copy(
            src_ref=exts[p].at[frames + f, lines], dst_ref=exts[p].at[f, lines],
            send_sem=t_send.at[p, f, c], recv_sem=t_recv.at[p, f, c],
            device_id={"tm": tm + 1}, device_id_type=MESH)

    def row_copy(p, f, down):
        src, dst, who = (rows, 0, ht + 1) if down else (1, rows + 1, ht - 1)
        return pltpu.make_async_remote_copy(
            src_ref=exts[p].at[f, src], dst_ref=exts[p].at[f, dst],
            send_sem=h_send.at[p, f, int(down)], recv_sem=h_recv.at[p, f, int(down)],
            device_id={"height": who}, device_id_type=MESH)

    def when_start(cond, copy):
        @pl.when(cond)
        def _():
            copy.start()

    def when_recv(cond, copy):
        @pl.when(cond)
        def _():
            copy.wait_recv()

    def when_sent(cond, copy):
        @pl.when(cond)
        def _():
            copy.wait_send()

    def send_part(p, f, c):
        if c == 0:
            when_start(has_up, row_copy(p, f + 2, False))
        if c == chunks - 1:
            when_start(has_down, row_copy(p, f + 2, True))
        if f >= frames - 2:
            when_start(has_next, time_copy(p, f - (frames - 2), c))

    def turn(p, w):
        square = (chans, chans)
        same = lax.broadcasted_iota(jnp.int32, square, 0) == lax.broadcasted_iota(jnp.int32, square, 1)
        identity = same.astype(jnp.float32).astype(jnp.bfloat16)

        @pl.loop(0, 3)
        def _(t):
            for k in range(3):
                taps = jnp.concatenate([w[t, j, k] for j in range(3)], axis=0)
                flipped = lax.dot_general(identity, taps, (((1,), (1,)), ((), ())), preferred_element_type=jnp.float32)
                turned[p, t, k * chans:(k + 1) * chans, :] = flipped.astype(jnp.bfloat16)

    def contrib(p, o, taps, first):
        ext, total = exts[p], None
        for t in taps:
            lines = [ext[o + t, i] for i in range(rows + 2)]
            block = jnp.concatenate([jnp.concatenate(lines[j:j + rows], axis=1) for j in range(3)], axis=0)
            part = jnp.dot(turned[p, t], block, preferred_element_type=jnp.float32)
            total = part if total is None else total + part
        if first:
            acc[o] = total
        else:
            acc[o] += total

    at_col = lax.broadcasted_iota(jnp.int32, (chans, width), 1)

    def combined(o, r, bias):
        cols = slice(r * width, (r + 1) * width)
        left = jnp.where(at_col == 0, 0.0, pltpu.roll(acc[o, 0:chans, cols], 1, 1))
        right = jnp.where(at_col == width - 1, 0.0, pltpu.roll(acc[o, 2 * chans:3 * chans, cols], width - 1, 1))
        return acc[o, chans:2 * chans, cols] + left + right + bias

    def convolve(p, finish, meanwhile=None):
        for f in range(2, frames + 2):
            when_recv(has_up, row_copy(p, f, True))
            when_recv(has_down, row_copy(p, f, False))
        for o in range(frames):
            contrib(p, o, tuple(t for t in range(3) if o + t >= 2), True)
        if meanwhile is not None:
            meanwhile()
        for o in range(2, frames):
            for c in range(chunks):
                finish(o, c)
        for f in (1, 0):
            for c in range(chunks):
                when_recv(has_prev, time_copy(p, f, c))
                if c == 0:
                    when_start(has_prev & has_up, row_copy(p, f, False))
                if c == chunks - 1:
                    when_start(has_prev & has_down, row_copy(p, f, True))
            when_recv(has_prev & has_up, row_copy(p, f, True))
            when_recv(has_prev & has_down, row_copy(p, f, False))
            for o in range(f, -1, -1):
                contrib(p, o, (f - o,), False)
                if o == f:
                    for c in range(chunks):
                        finish(o, c)

    for copy in small:
        copy.wait()
    square = (chans, chans)
    diagonal = lax.broadcasted_iota(jnp.int32, square, 0) == lax.broadcasted_iota(jnp.int32, square, 1)
    gain1, bias1, gain2, bias2 = [
        jnp.sum(jnp.where(diagonal, vecs[i], 0.0), axis=1, keepdims=True) for i in range(4)
    ]
    for f in range(frames):
        @pl.loop(0, rows)
        def _(r, f=f):
            ext1[f + 2, r + 1] = normalize(x_ref[f, r].astype(jnp.float32), gain1)

    pl.semaphore_wait(barrier, sum(there.astype(jnp.int32) for there, _ in sides))
    for f in range(frames - 1, -1, -1):
        for c in range(chunks):
            send_part(0, f, c)

    def finish_first(o, c):
        for r in range(c * CHUNK, (c + 1) * CHUNK):
            ext2[o + 2, r + 1] = normalize(combined(o, r, bias1), gain2)
        send_part(1, o, c)

    def finish_second(o, c):
        for r in range(c * CHUNK, (c + 1) * CHUNK):
            o_ref[o, r] = (x_ref[o, r].astype(jnp.float32) + combined(o, r, bias2)).astype(jnp.bfloat16)

    load1.wait()
    load2.start()
    turn(0, w1)
    other_chip = has_prev & (lax.rem(tm, 2) == 0)

    def turn_second():
        load2.wait()

        @pl.when(other_chip)
        def _():
            turn(1, w2)

    convolve(0, finish_first, turn_second)

    @pl.when(jnp.logical_not(other_chip))
    def _():
        turn(1, w2)

    convolve(1, finish_second)

    for p in range(2):
        for f in range(2):
            for c in range(chunks):
                when_sent(has_next, time_copy(p, f, c))
        for f in range(frames + 2):
            extra = has_prev if f < 2 else True
            when_sent(has_up & extra, row_copy(p, f, False))
            when_sent(has_down & extra, row_copy(p, f, True))


def local(tms, heights, hidden_in, gain_first, weight_first, bias_first, gain_second, weight_second, bias_second):
    frames, rows, width, chans = hidden_in.shape
    chunks = rows // CHUNK
    vmem = pl.BlockSpec(memory_space=pltpu.VMEM)
    hbm = pl.BlockSpec(memory_space=pl.ANY)
    ext = pltpu.VMEM((frames + 2, rows + 2, chans, width), jnp.bfloat16)
    weight = pltpu.VMEM(weight_first.shape, jnp.bfloat16)
    dma = pltpu.SemaphoreType.DMA
    flops = 2 * 2 * frames * rows * width * 27 * chans * chans
    turned_in = jnp.swapaxes(hidden_in, 2, 3)
    result = pl.pallas_call(
        functools.partial(kernel, tms, heights),
        out_shape=jax.ShapeDtypeStruct(turned_in.shape, jnp.bfloat16),
        in_specs=[vmem] + [hbm] * 6,
        out_specs=vmem,
        scratch_shapes=[
            ext,
            ext,
            pltpu.VMEM((frames, 3 * chans, rows * width), jnp.float32),
            weight,
            weight,
            pltpu.VMEM((2, 3, 3 * chans, 3 * chans), jnp.bfloat16),
            pltpu.VMEM((4, 1, chans), jnp.float32),
            dma((4,)),
            dma((2,)),
            dma((2, 2, chunks)),
            dma((2, 2, chunks)),
            dma((2, frames + 2, 2)),
            dma((2, frames + 2, 2)),
        ],
        compiler_params=pltpu.CompilerParams(
            collective_id=0, has_side_effects=True, vmem_limit_bytes=56 * 2**20
        ),
        cost_estimate=pl.CostEstimate(flops=flops, bytes_accessed=8 * 2**20, transcendentals=0),
    )(
        turned_in,
        gain_first.reshape(1, chans),
        bias_first.reshape(1, chans),
        gain_second.reshape(1, chans),
        bias_second.reshape(1, chans),
        weight_first,
        weight_second,
    )
    return jnp.swapaxes(result, 2, 3)


def solution(mesh):
    in_specs = (P("tm", "height", None, None), P(), P(), P(), P(), P(), P())
    out_specs = P("tm", "height", None, None)
    body = functools.partial(local, mesh.shape["tm"], mesh.shape["height"])
    return jax.shard_map(body, mesh=mesh, in_specs=in_specs, out_specs=out_specs, check_vma=False)
```

```python
import functools

import jax
import jax.numpy as jnp
from jax import lax
from jax.experimental import pallas as pl
from jax.experimental.pallas import tpu as pltpu
from jax.sharding import PartitionSpec as P

epsilon = 1e-06
MESH = pl.DeviceIdType.MESH
CHUNK = 4


def normalize(values, gain):
    scaled = values * lax.rsqrt(jnp.mean(values * values, axis=0, keepdims=True) + epsilon) * gain
    return jax.nn.silu(scaled).astype(jnp.bfloat16)


def kernel(
    tms, heights, x_ref, g1_ref, b1_ref, g2_ref, b2_ref, w1_hbm, w2_hbm, o_ref,
    ext1, ext2, acc, w1, w2, turned, vecs, vsem, wsem, t_send, t_recv, h_send, h_recv, c_send,
):
    frames, rows, chans, width = x_ref.shape
    chunks = rows // CHUNK
    tm, ht = lax.axis_index("tm"), lax.axis_index("height")
    has_prev, has_next = tm > 0, tm < tms - 1
    other_chip = has_prev & (lax.rem(tm, 2) == 0)
    to_core = has_next & (lax.rem(tm, 2) == 0)
    has_up, has_down = ht > 0, ht < heights - 1

    load1 = pltpu.make_async_copy(w1_hbm, w1, wsem.at[0])
    load2 = pltpu.make_async_copy(w2_hbm, w2, wsem.at[1])
    load1.start()
    small = [pltpu.make_async_copy(ref, vecs.at[i], vsem.at[i]) for i, ref in enumerate((g1_ref, b1_ref, g2_ref, b2_ref))]
    for copy in small:
        copy.start()

    barrier = pltpu.get_barrier_semaphore()
    sides = ((has_prev, {"tm": tm - 1}), (has_next, {"tm": tm + 1}), (has_up, {"height": ht - 1}), (has_down, {"height": ht + 1}))
    for there, who in sides:
        @pl.when(there)
        def _(who=who):
            pl.semaphore_signal(barrier, inc=1, device_id=who, device_id_type=MESH)

    zeros_row = jnp.zeros((chans, width), jnp.bfloat16)
    for ext in (ext1, ext2):
        @pl.when(jnp.logical_not(has_prev))
        def _(ext=ext):
            for f in range(2):
                @pl.loop(0, rows + 2)
                def _(r, f=f):
                    ext[f, r] = zeros_row

        @pl.when(jnp.logical_not(has_up))
        def _(ext=ext):
            for f in range(frames + 2):
                ext[f, 0] = zeros_row

        @pl.when(jnp.logical_not(has_down))
        def _(ext=ext):
            for f in range(frames + 2):
                ext[f, rows + 1] = zeros_row


    exts = (ext1, ext2)

    def time_copy(p, f, c):
        lines = pl.ds(1 + c * CHUNK, CHUNK)
        return pltpu.make_async_remote_copy(
            src_ref=exts[p].at[frames + f, lines], dst_ref=exts[p].at[f, lines],
            send_sem=t_send.at[p, f, c], recv_sem=t_recv.at[p, f, c],
            device_id={"tm": tm + 1}, device_id_type=MESH)

    def row_copy(p, f, down):
        src, dst, who = (rows, 0, ht + 1) if down else (1, rows + 1, ht - 1)
        return pltpu.make_async_remote_copy(
            src_ref=exts[p].at[f, src], dst_ref=exts[p].at[f, dst],
            send_sem=h_send.at[p, f, int(down)], recv_sem=h_recv.at[p, f, int(down)],
            device_id={"height": who}, device_id_type=MESH)

    def corner_copy(p, f, down):
        line = 0 if down else rows + 1
        return pltpu.make_async_remote_copy(
            src_ref=exts[p].at[frames + f, line], dst_ref=exts[p].at[f, line],
            send_sem=c_send.at[p, f, int(down)], recv_sem=h_recv.at[p, f, int(down)],
            device_id={"tm": tm + 1}, device_id_type=MESH)

    def when_start(cond, copy):
        @pl.when(cond)
        def _():
            copy.start()

    def when_recv(cond, copy):
        @pl.when(cond)
        def _():
            copy.wait_recv()

    def when_sent(cond, copy):
        @pl.when(cond)
        def _():
            copy.wait_send()

    def send_part(p, f, c):
        if c == 0:
            when_start(has_up, row_copy(p, f + 2, False))
        if c == chunks - 1:
            when_start(has_down, row_copy(p, f + 2, True))
        if f >= frames - 2:
            when_start(has_next, time_copy(p, f - (frames - 2), c))

    def turn(p, w):
        square = (chans, chans)
        same = lax.broadcasted_iota(jnp.int32, square, 0) == lax.broadcasted_iota(jnp.int32, square, 1)
        identity = same.astype(jnp.float32).astype(jnp.bfloat16)

        @pl.loop(0, 3)
        def _(t):
            for k in range(3):
                taps = jnp.concatenate([w[t, j, k] for j in range(3)], axis=0)
                flipped = lax.dot_general(identity, taps, (((1,), (1,)), ((), ())), preferred_element_type=jnp.float32)
                turned[p, t, k * chans:(k + 1) * chans, :] = flipped.astype(jnp.bfloat16)

    def contrib(p, o, taps, first):
        ext, total = exts[p], None
        for t in taps:
            lines = [ext[o + t, i] for i in range(rows + 2)]
            block = jnp.concatenate([jnp.concatenate(lines[j:j + rows], axis=1) for j in range(3)], axis=0)
            part = jnp.dot(turned[p, t], block, preferred_element_type=jnp.float32)
            total = part if total is None else total + part
        if first:
            acc[o] = total
        else:
            acc[o] += total

    at_col = lax.broadcasted_iota(jnp.int32, (chans, width), 1)

    def combined(o, r, bias):
        cols = slice(r * width, (r + 1) * width)
        left = jnp.where(at_col == 0, 0.0, pltpu.roll(acc[o, 0:chans, cols], 1, 1))
        right = jnp.where(at_col == width - 1, 0.0, pltpu.roll(acc[o, 2 * chans:3 * chans, cols], width - 1, 1))
        return acc[o, chans:2 * chans, cols] + left + right + bias

    def convolve(p, finish, meanwhile=None):
        for f in range(2, frames + 2):
            when_recv(has_up, row_copy(p, f, True))
            when_recv(has_down, row_copy(p, f, False))
        for f in (1, 0):
            when_start(to_core & has_up, corner_copy(p, f, True))
            when_start(to_core & has_down, corner_copy(p, f, False))
        for o in range(frames):
            contrib(p, o, tuple(t for t in range(3) if o + t >= 2), True)
        if meanwhile is not None:
            meanwhile()
        for o in range(2, frames):
            for c in range(chunks):
                finish(o, c)
        def arrive(f):
            for c in range(chunks):
                when_recv(has_prev, time_copy(p, f, c))
                if c == 0:
                    when_start(other_chip & has_up, row_copy(p, f, False))
                if c == chunks - 1:
                    when_start(other_chip & has_down, row_copy(p, f, True))

        def corners(f):
            when_recv(has_prev & has_up, row_copy(p, f, True))
            when_recv(has_prev & has_down, row_copy(p, f, False))

        arrive(1)
        corners(1)
        contrib(p, 1, (0,), False)
        for c in range(chunks):
            finish(1, c)
        arrive(0)
        contrib(p, 0, (1,), False)
        corners(0)
        contrib(p, 0, (0,), False)
        for c in range(chunks):
            finish(0, c)

    for copy in small:
        copy.wait()
    square = (chans, chans)
    diagonal = lax.broadcasted_iota(jnp.int32, square, 0) == lax.broadcasted_iota(jnp.int32, square, 1)
    gain1, bias1, gain2, bias2 = [
        jnp.sum(jnp.where(diagonal, vecs[i], 0.0), axis=1, keepdims=True) for i in range(4)
    ]
    for f in range(frames):
        @pl.loop(0, rows)
        def _(r, f=f):
            ext1[f + 2, r + 1] = normalize(x_ref[f, r].astype(jnp.float32), gain1)

    pl.semaphore_wait(barrier, sum(there.astype(jnp.int32) for there, _ in sides))
    for f in range(frames - 1, -1, -1):
        for c in range(chunks):
            send_part(0, f, c)

    def finish_first(o, c):
        for r in range(c * CHUNK, (c + 1) * CHUNK):
            ext2[o + 2, r + 1] = normalize(combined(o, r, bias1), gain2)
        send_part(1, o, c)

    def finish_second(o, c):
        for r in range(c * CHUNK, (c + 1) * CHUNK):
            o_ref[o, r] = (x_ref[o, r].astype(jnp.float32) + combined(o, r, bias2)).astype(jnp.bfloat16)

    load1.wait()
    load2.start()
    turn(0, w1)

    def turn_second():
        load2.wait()

        @pl.when(other_chip)
        def _():
            turn(1, w2)

    convolve(0, finish_first, turn_second)

    @pl.when(jnp.logical_not(other_chip))
    def _():
        turn(1, w2)

    convolve(1, finish_second)

    for p in range(2):
        for f in range(2):
            for c in range(chunks):
                when_sent(has_next, time_copy(p, f, c))
        for f in range(2):
            when_sent(to_core & has_up, corner_copy(p, f, True))
            when_sent(to_core & has_down, corner_copy(p, f, False))
        for f in range(frames + 2):
            extra = other_chip if f < 2 else True
            when_sent(has_up & extra, row_copy(p, f, False))
            when_sent(has_down & extra, row_copy(p, f, True))


def local(tms, heights, hidden_in, gain_first, weight_first, bias_first, gain_second, weight_second, bias_second):
    frames, rows, width, chans = hidden_in.shape
    chunks = rows // CHUNK
    vmem = pl.BlockSpec(memory_space=pltpu.VMEM)
    hbm = pl.BlockSpec(memory_space=pl.ANY)
    ext = pltpu.VMEM((frames + 2, rows + 2, chans, width), jnp.bfloat16)
    weight = pltpu.VMEM(weight_first.shape, jnp.bfloat16)
    dma = pltpu.SemaphoreType.DMA
    flops = 2 * 2 * frames * rows * width * 27 * chans * chans
    turned_in = jnp.swapaxes(hidden_in, 2, 3)
    result = pl.pallas_call(
        functools.partial(kernel, tms, heights),
        out_shape=jax.ShapeDtypeStruct(turned_in.shape, jnp.bfloat16),
        in_specs=[vmem] + [hbm] * 6,
        out_specs=vmem,
        scratch_shapes=[
            ext,
            ext,
            pltpu.VMEM((frames, 3 * chans, rows * width), jnp.float32),
            weight,
            weight,
            pltpu.VMEM((2, 3, 3 * chans, 3 * chans), jnp.bfloat16),
            pltpu.VMEM((4, 1, chans), jnp.float32),
            dma((4,)),
            dma((2,)),
            dma((2, 2, chunks)),
            dma((2, 2, chunks)),
            dma((2, frames + 2, 2)),
            dma((2, frames + 2, 2)),
            dma((2, 2, 2)),
        ],
        compiler_params=pltpu.CompilerParams(
            collective_id=0, has_side_effects=True, vmem_limit_bytes=56 * 2**20
        ),
        cost_estimate=pl.CostEstimate(flops=flops, bytes_accessed=8 * 2**20, transcendentals=0),
    )(
        turned_in,
        gain_first.reshape(1, chans),
        bias_first.reshape(1, chans),
        gain_second.reshape(1, chans),
        bias_second.reshape(1, chans),
        weight_first,
        weight_second,
    )
    return jnp.swapaxes(result, 2, 3)


def solution(mesh):
    in_specs = (P("tm", "height", None, None), P(), P(), P(), P(), P(), P())
    out_specs = P("tm", "height", None, None)
    body = functools.partial(local, mesh.shape["tm"], mesh.shape["height"])
    return jax.shard_map(body, mesh=mesh, in_specs=in_specs, out_specs=out_specs, check_vma=False)
```
